512 devices in a mesh: dp: 4 (over z_hi), cin: 32 (over y, x, core), cout: 4 (over z_lo).
Axes of the slice: x: 4, y: 4, z: 16 (z_hi: 4, z_lo: 4; z = z_hi * 4 + z_lo), core: 2. Of those that a mesh axis runs over, the one named last changes fastest.
Arguments:
- weight: bfloat16 [8, 2, 2048, 2048], P(None, None, 'cin', 'cout'), may hold values from -0.09375 to 0.09375
- spectrum: bfloat16 [8, 2, 2048, 2048], P(None, None, ('cin', 'cout'), 'dp'), may hold values from -0.1796875 to 0.1796875
- out_grad: bfloat16 [8, 2, 2048, 2048], P(None, None, ('cout', 'cin'), 'dp'), may hold values from -6 to 6
Outputs:
- spectrum_grad: bfloat16 [8, 2, 2048, 2048], P(None, None, ('cin', 'cout'), 'dp')
- weight_grad: bfloat16 [8, 2, 2048, 2048], P(None, None, 'cin', 'cout')
The draws below stay inside these ranges and needn't reach their ends.
All inputs are finite; a program needn't handle non-finite values.
Results may differ from the reference program's by a relative error of at most 0.001.
Values may be sent and summed in bfloat16 or wider, within the bound.
No kernel may reach another device: no remote copies, remote signals or barrier semaphores. Data moves between devices by JAX's collectives and lax.ppermute only.
A program may use at most 64 MiB of HBM per device.

```python
import jax
import jax.numpy as jnp
from jax import lax

C = 2048
MODES = 8
BATCH = 2048


def block_levels(rng, extent, split, smallest, high):
    gain = 1.0
    for dim, shards_of in split:
        heights = jax.random.uniform(jax.random.fold_in(jax.random.fold_in(rng, 6), dim), (shards_of,), jnp.float32, smallest / len(split), high / len(split))
        gain = gain * jnp.repeat(jnp.exp(heights), extent[dim] // shards_of).reshape((-1,) + (1,) * (len(extent) - 1 - dim))
    return gain


def normal_values(rng, shape, deviation, bound, shards=(), held_as=jnp.bfloat16):
    drawn = deviation * jax.random.normal(rng, shape, jnp.float32)
    if shards:
        drawn = drawn * block_levels(rng, shape, shards, -0.22, 0.18)
    return jnp.clip(drawn, -bound, bound).astype(held_as)


def setup_inputs(seed: int = 0) -> dict:
    splits = jax.random.split(jax.random.key(seed), 4)
    return {
        "weight": normal_values(splits[0], (MODES, 2, C, C), (2 * C) ** -0.5, 0.09375, ((2, 32), (3, 4))),
        "spectrum": normal_values(splits[1], (MODES, 2, C, BATCH), 0.03, 0.1796875, ((2, 128), (3, 4))),
        "out_grad": normal_values(splits[2], (MODES, 2, C, BATCH), 1.0, 6.0, ((2, 128), (3, 4))),
    }


def mode_grads(inputs):
    weight_mode, spec_mode, grad_mode = inputs
    w_real = weight_mode[0]
    w_imag = weight_mode[1]
    x_real = spec_mode[0]
    x_imag = spec_mode[1]
    g_real = grad_mode[0]
    g_imag = grad_mode[1]
    dx_real = jnp.dot(w_real, g_real, preferred_element_type=jnp.float32) + jnp.dot(w_imag, g_imag, preferred_element_type=jnp.float32)
    dx_imag = jnp.dot(w_real, g_imag, preferred_element_type=jnp.float32) - jnp.dot(w_imag, g_real, preferred_element_type=jnp.float32)
    dw_real = jnp.dot(x_real, g_real.T, preferred_element_type=jnp.float32) + jnp.dot(x_imag, g_imag.T, preferred_element_type=jnp.float32)
    dw_imag = jnp.dot(x_real, g_imag.T, preferred_element_type=jnp.float32) - jnp.dot(x_imag, g_real.T, preferred_element_type=jnp.float32)
    spec_out = jnp.stack([dx_real, dx_imag]).astype(jnp.bfloat16)
    weight_out = jnp.stack([dw_real, dw_imag]).astype(jnp.bfloat16)
    return spec_out, weight_out


def reference(weight, spectrum, out_grad):
    spectrum_grad, weight_grad = lax.map(mode_grads, (weight, spectrum, out_grad))
    return spectrum_grad, weight_grad
```

```python
import functools

import jax
import jax.numpy as jnp
from jax import lax
from jax.experimental import pallas as pl
from jax.experimental.pallas import tpu as pltpu
from jax.sharding import PartitionSpec as P

HEARD = (0, 3, 1, 2)
SHIFTS = (1, 3, 2)
MIB = 1 << 20
ANY = pl.BlockSpec(memory_space=pl.ANY)
SMEM = pl.BlockSpec(memory_space=pltpu.SMEM)
VMEM = pl.BlockSpec(memory_space=pltpu.VMEM)


def ring(value, axis, shift):
    return lax.ppermute(value, axis, [(i, (i + shift) % 4) for i in range(4)])


def flip(value, axis, bits, size=4):
    return lax.ppermute(value, axis, [(i, i ^ bits) for i in range(size)])


def swap_cores(value):
    return flip(value, "cin", 1, 32)


def hop(value, shift, stage):
    pairs = []
    for i in range(32):
        y, x, core = i // 8, (i // 2) % 4, i % 2
        if core == stage:
            x = (x + shift) % 4
        else:
            y = (y + shift) % 4
        pairs.append((i, (y * 4 + x) * 2 + core))
    return lax.ppermute(value, "cin", pairs)


def plane_gather(mine, theirs):
    first = jnp.stack([mine, swap_cores(theirs)])
    line = jnp.stack([first] + [hop(first, shift, 0) for shift in SHIFTS])
    held = [line] + [hop(line, shift, 1) for shift in SHIFTS]
    return held, [swap_cores(piece) for piece in held]


def plane_blocks():
    place = lax.axis_index("cin")
    y, x, core = place // 8, (place // 2) % 4, place % 2
    heard = jnp.array(HEARD, jnp.int32)
    tables = []
    for owner in (core, 1 - core):
        along_x = (x + heard) % 4
        along_y = (y + heard) % 4
        second, first, source = jnp.meshgrid(
            jnp.arange(4), jnp.arange(4), jnp.arange(2), indexing="ij"
        )
        across = jnp.where(owner == 0, along_x[first], along_x[second])
        down = jnp.where(owner == 0, along_y[second], along_y[first])
        origin = jnp.where(source == 0, owner, 1 - owner)
        tables.append(((down * 4 + across) * 2 + origin).astype(jnp.int32).reshape(32))
    return jnp.stack(tables)


def input_terms(half, blocks, scalars, w, p0, p1, p2, p3, keep, send, grads, sem):
    pieces = (p0, p1, p2, p3)
    for second in range(4):
        for first in range(4):
            for source in range(2):
                row = pl.multiple_of(blocks[half, (second * 4 + first) * 2 + source] * 16, 16)
                pltpu.make_async_copy(
                    pieces[second].at[first, source], grads.at[:, :, pl.ds(row, 16), :], sem
                ).start()
    pltpu.make_async_copy(grads, grads, sem).wait()
    base = scalars[half]
    rows = [pl.multiple_of(scalars[2 + r], 16) for r in range(4)]
    for mode in range(4):
        real = jnp.concatenate([w[base + mode, 0, pl.ds(row, 16), :] for row in rows], axis=0)
        imag = jnp.concatenate([w[base + mode, 1, pl.ds(row, 16), :] for row in rows], axis=0)
        total = jnp.dot(
            jnp.concatenate([real, -imag], axis=0), grads[mode, 0], preferred_element_type=jnp.float32
        ) + jnp.dot(
            jnp.concatenate([imag, real], axis=0), grads[mode, 1], preferred_element_type=jnp.float32
        )
        for part in range(2):
            for r in range(2):
                start = part * 64 + r * 16
                keep[r, mode, part] = total[start : start + 16]
                send[r, mode, part] = total[start + 32 : start + 48]


def input_half(half, blocks, scalars, weight, held):
    out = jax.ShapeDtypeStruct((2, 4, 2, 16, 512), jnp.float32)
    return pl.pallas_call(
        functools.partial(input_terms, half),
        out_shape=(out, out),
        in_specs=[SMEM, SMEM, VMEM] + [ANY] * 4,
        out_specs=(VMEM, VMEM),
        scratch_shapes=[pltpu.VMEM((4, 2, 512, 512), jnp.bfloat16), pltpu.SemaphoreType.DMA],
        compiler_params=pltpu.CompilerParams(vmem_limit_bytes=20 * MIB),
        cost_estimate=pl.CostEstimate(flops=1 << 30, bytes_accessed=7 * MIB, transcendentals=0),
        name="input_terms",
    )(blocks, scalars, weight, *held)


def weight_terms(slot, blocks, scalars, *refs):
    own, other, late, xs, out, grads, rows, sem = refs[:4], refs[4:8], refs[8:12], refs[12:15], *refs[15:]
    mode = scalars[6 + slot]
    near = scalars[8 + slot]

    def place(half, index):
        return pl.ds(pl.multiple_of(blocks[half, index] * 16, 16), 16)

    for second in range(4):
        for first in range(4):
            for source in range(2):
                index = (second * 4 + first) * 2 + source
                pltpu.make_async_copy(
                    late[second].at[first, source], grads.at[pl.ds(1, 3), :, place(slot, index), :], sem
                ).start()

    def local(half, pieces):
        for second in range(4):
            for first in range(4):
                for source in range(2):
                    index = (second * 4 + first) * 2 + source
                    pltpu.make_async_copy(
                        pieces[second].at[first, source, near], grads.at[0, :, place(half, index), :], sem
                    ).start()

    @pl.when(scalars[10] == 0)
    def _():
        local(0, own)

    @pl.when(scalars[10] != 0)
    def _():
        local(1, other)

    for index, piece in enumerate((xs[0], xs[1], xs[2].at[0], xs[2].at[1])):
        row = pl.multiple_of(scalars[11 + index], 16)
        for block in range(4):
            pltpu.make_async_copy(
                piece.at[block, mode], rows.at[block, :, pl.ds(row, 16), :], sem
            ).start()
    pltpu.make_async_copy(grads, grads, sem).wait()
    pltpu.make_async_copy(rows, rows, sem).wait()

    total = jnp.zeros((128, 512), jnp.float32)
    contract = (((1,), (1,)), ((), ()))
    for block in range(4):
        real = rows[block, 0]
        imag = rows[block, 1]
        total += lax.dot_general(
            jnp.concatenate([real, -imag], axis=0), grads[block, 0], contract, preferred_element_type=jnp.float32
        )
        total += lax.dot_general(
            jnp.concatenate([imag, real], axis=0), grads[block, 1], contract, preferred_element_type=jnp.float32
        )
    out[0] = total[:64].astype(jnp.bfloat16)
    out[1] = total[64:].astype(jnp.bfloat16)


def weight_mode(slot, blocks, scalars, own, other, late, xs):
    return pl.pallas_call(
        functools.partial(weight_terms, slot),
        out_shape=jax.ShapeDtypeStruct((2, 64, 512), jnp.bfloat16),
        in_specs=[SMEM, SMEM] + [ANY] * 15,
        out_specs=VMEM,
        scratch_shapes=[
            pltpu.VMEM((4, 2, 512, 512), jnp.bfloat16),
            pltpu.VMEM((4, 2, 64, 512), jnp.bfloat16),
            pltpu.SemaphoreType.DMA,
        ],
        compiler_params=pltpu.CompilerParams(vmem_limit_bytes=20 * MIB),
        cost_estimate=pl.CostEstimate(flops=1 << 30, bytes_accessed=5 * MIB, transcendentals=0),
        name="weight_terms",
    )(blocks, scalars, *own, *other, *late, *xs)


def place_modes(scalars, *refs):
    out, sem = refs[-2:]
    copies = []
    for slot in range(2):
        mine, back, ahead, far_real, far_imag = refs[5 * slot : 5 * slot + 5]
        for source, step in ((mine, 0), (back, 1), (ahead, 2)):
            copies.append((source, out.at[scalars[15 + 4 * slot + step]]))
        far = scalars[15 + 4 * slot + 3]
        copies.append((far_real, out.at[far, 0]))
        copies.append((far_imag, out.at[far, 1]))
    for source, target in copies:
        pltpu.make_async_copy(source, target, sem).start()
    pltpu.make_async_copy(out, out, sem).wait()


def on_device(weight, spectrum, out_grad):
    dp, place, cout = lax.axis_index("dp"), lax.axis_index("cin"), lax.axis_index("cout")
    core = place % 2
    blocks = plane_blocks()
    slots = (core, 1 - core)
    scalars = jnp.stack(
        [4 * core, 4 - 4 * core]
        + [16 * (cout ^ r) for r in (0, 2, 1, 3)]
        + list(slots)
        + [(2 * dp + slot) % 4 for slot in slots]
        + [(dp // 2) ^ core]
        + [16 * (cout ^ r) for r in (0, 2, 1, 3)]
        + [2 * ((dp + step) % 4) + slot for slot in slots for step in HEARD]
    ).astype(jnp.int32)

    def modes_of(value, start, count):
        return lax.dynamic_slice_in_dim(value, start, count, 0)

    with jax.named_scope("exchange_modes"):
        exchanged = []
        for shift in SHIFTS:
            start = 2 * ((dp + shift) % 4)
            packed = jnp.stack([modes_of(spectrum, start, 2), modes_of(out_grad, start, 2)])
            exchanged.append(ring(packed, "dp", shift))

    with jax.named_scope("gather_grad"):
        own, other = plane_gather(modes_of(out_grad, 4 * core, 4), modes_of(out_grad, 4 - 4 * core, 4))

    with jax.named_scope("gather_rows"):
        xs = jnp.stack([modes_of(spectrum, 2 * dp, 2)] + [block[0] for block in exchanged])
        xs_across = flip(xs, "cout", 2)
        xs_beside = flip(jnp.stack([xs, xs_across]), "cout", 1)

    with jax.named_scope("gather_late_grad"):
        late = jnp.stack([block[1] for block in exchanged], axis=1)
        late_own, late_other = plane_gather(
            modes_of(late, core, 1)[0], modes_of(late, 1 - core, 1)[0]
        )

    halves = []
    for half, held in enumerate((own, other)):
        keep, send = input_half(half, blocks, scalars, weight, held)
        with jax.named_scope("sum_input"):
            beside = flip(send, "cout", 1)
            across = flip(keep[1] + beside[1], "cout", 2)
            halves.append(((keep[0] + beside[0]) + across).astype(jnp.bfloat16))
    spectrum_grad = jnp.concatenate(
        [jnp.where(core == 0, halves[0], halves[1]), jnp.where(core == 0, halves[1], halves[0])], axis=0
    )

    parts = []
    for slot, held in enumerate((late_own, late_other)):
        mine = weight_mode(slot, blocks, scalars, own, other, held, (xs, xs_across, xs_beside))
        with jax.named_scope("spread_weight"):
            back, ahead = ring(mine, "dp", 1), ring(mine, "dp", 3)
            parts += [mine, back, ahead, ring(back[0], "dp", 1), ring(ahead[1], "dp", 3)]
    weight_grad = pl.pallas_call(
        place_modes,
        out_shape=jax.ShapeDtypeStruct(weight.shape, jnp.bfloat16),
        in_specs=[SMEM] + [ANY] * 10,
        out_specs=ANY,
        scratch_shapes=[pltpu.SemaphoreType.DMA],
        cost_estimate=pl.CostEstimate(flops=0, bytes_accessed=2 * MIB, transcendentals=0),
        name="place_modes",
    )(scalars, *parts)
    return (spectrum_grad, weight_grad)


def solution(mesh):
    placed = (
        P(None, None, "cin", "cout"),
        P(None, None, ("cin", "cout"), "dp"),
        P(None, None, ("cout", "cin"), "dp"),
    )
    return jax.shard_map(
        on_device,
        mesh=mesh,
        in_specs=placed,
        out_specs=(P(None, None, ("cin", "cout"), "dp"), P(None, None, "cin", "cout")),
        check_vma=False,
    )
```

```python
import jax
import jax.numpy as jnp
from jax import lax
from jax.experimental import pallas as pl
from jax.experimental.pallas import tpu as pltpu
from jax.sharding import PartitionSpec as P

HEARD = (0, 3, 1, 2)
SHIFTS = (1, 3, 2)
TREE = (0, 2, 1, 3)
MIB = 1 << 20
ANY = pl.BlockSpec(memory_space=pl.ANY)
SMEM = pl.BlockSpec(memory_space=pltpu.SMEM)
VMEM = pl.BlockSpec(memory_space=pltpu.VMEM)


def ring(value, axis, shift):
    return lax.ppermute(value, axis, [(i, (i + shift) % 4) for i in range(4)])


def flip(value, axis, bits, size=4):
    return lax.ppermute(value, axis, [(i, i ^ bits) for i in range(size)])


def swap_cores(value):
    return flip(value, "cin", 1, 32)


def hop(value, shift, stage):
    pairs = []
    for i in range(32):
        y, x, core = i // 8, (i // 2) % 4, i % 2
        if core == stage:
            x = (x + shift) % 4
        else:
            y = (y + shift) % 4
        pairs.append((i, (y * 4 + x) * 2 + core))
    return lax.ppermute(value, "cin", pairs)


def plane_blocks(y, x, core):
    heard = jnp.array(HEARD, jnp.int32)
    along_x = (x + heard) % 4
    along_y = (y + heard) % 4
    blocks = []
    for second in range(4):
        for first in range(4):
            for source in range(2):
                across = jnp.where(core == 0, along_x[first], along_x[second])
                down = jnp.where(core == 0, along_y[second], along_y[first])
                blocks.append((down * 4 + across) * 2 + (core ^ source))
    return blocks


def fetch_plane(blocks, pieces, target, sem):
    for second in range(4):
        for first in range(4):
            for source in range(2):
                row = pl.multiple_of(blocks[(second * 4 + first) * 2 + source] * 16, 16)
                pltpu.make_async_copy(
                    pieces[second](first, source), target(pl.ds(row, 16)), sem
                ).start()


def input_terms(blocks, scalars, w, w_other, p0, p1, p2, p3, keep, send, grads, sem):
    fetch_plane(
        blocks,
        [lambda first, source, p=p: p.at[first, source] for p in (p0, p1, p2, p3)],
        lambda rows: grads.at[:, :, rows, :],
        sem,
    )
    base = scalars[0]
    rows = [pl.ds(pl.multiple_of(scalars[2 + r], 16), 16) for r in range(4)]
    pltpu.make_async_copy(grads, grads, sem).wait()
    for mode in range(4):
        real, imag = (
            jnp.concatenate(
                [block for row in rows for block in (w[base + mode, part, row, :], w_other[mode, part, row, :])],
                axis=0,
            )
            for part in range(2)
        )
        total = jnp.dot(
            jnp.concatenate([real, -imag], axis=0), grads[mode, 0], preferred_element_type=jnp.float32
        ) + jnp.dot(
            jnp.concatenate([imag, real], axis=0), grads[mode, 1], preferred_element_type=jnp.float32
        )
        total = total.reshape(2, 4, 2, 16, 512)
        for part in range(2):
            for r in range(2):
                keep[r, mode, part] = total[part, r]
                send[r, mode, part] = total[part, r + 2]


def weight_terms(blocks, scalars, p0, p1, p2, p3, l0, l1, l2, l3, x0, x1, x2, out, grads, rows, sem):
    mode = scalars[1]
    fetch_plane(
        blocks,
        [lambda first, source, p=p: p.at[first, source, mode] for p in (p0, p1, p2, p3)],
        lambda place: grads.at[0, :, place, :],
        sem,
    )
    for index, piece in enumerate((x0, x1, x2.at[0], x2.at[1])):
        for source in range(2):
            row = pl.multiple_of(scalars[2 + index] + 64 * source, 16)
            pltpu.make_async_copy(piece.at[source], rows.at[:, :, pl.ds(row, 16), :], sem).start()
    fetch_plane(
        blocks,
        [lambda first, source, p=p: p.at[first, source] for p in (l0, l1, l2, l3)],
        lambda place: grads.at[pl.ds(1, 3), :, place, :],
        sem,
    )
    pltpu.make_async_copy(grads, grads, sem).wait()
    pltpu.make_async_copy(rows, rows, sem).wait()

    total = jnp.zeros((256, 512), jnp.float32)
    contract = (((1,), (1,)), ((), ()))
    for block in range(4):
        real = rows[block, 0]
        imag = rows[block, 1]
        total += lax.dot_general(
            jnp.concatenate([real, -imag], axis=0), grads[block, 0], contract, preferred_element_type=jnp.float32
        )
        total += lax.dot_general(
            jnp.concatenate([imag, real], axis=0), grads[block, 1], contract, preferred_element_type=jnp.float32
        )
    for part in range(2):
        for source in range(2):
            start = part * 128 + source * 64
            out[source, part] = total[start : start + 64].astype(jnp.bfloat16)


def place_modes(scalars, own, back, ahead, far, out, sem):
    for step, piece in enumerate((own, back, ahead, far)):
        for slot in range(2):
            pltpu.make_async_copy(piece.at[slot], out.at[scalars[6 + 2 * step + slot]], sem).start()
    pltpu.make_async_copy(out, out, sem).wait()


def on_device(weight, spectrum, out_grad):
    dp, place, cout = lax.axis_index("dp"), lax.axis_index("cin"), lax.axis_index("cout")
    core = place % 2
    blocks = jnp.stack(plane_blocks(place // 8, (place // 2) % 4, core)).astype(jnp.int32)
    scalars = jnp.stack(
        [4 * core, dp]
        + [16 * (cout ^ r) for r in TREE]
        + [4 * (core ^ slot) + (dp + step) % 4 for step in HEARD for slot in range(2)]
    ).astype(jnp.int32)

    def modes_of(value, start, count):
        return lax.dynamic_slice_in_dim(value, start, count, 0)

    mine, theirs = 4 * core, 4 - 4 * core
    with jax.named_scope("swap_modes"):
        packed = swap_cores(jnp.stack([modes_of(spectrum, theirs, 4), modes_of(out_grad, theirs, 4)]))
        w_other = swap_cores(modes_of(weight, theirs, 4))
        spec = jnp.stack([modes_of(spectrum, mine, 4), packed[0]])
        grad = jnp.stack([modes_of(out_grad, mine, 4), packed[1]])

    with jax.named_scope("gather_grad"):
        line = jnp.stack([grad] + [hop(grad, shift, 0) for shift in SHIFTS])
        held = [line] + [hop(line, shift, 1) for shift in SHIFTS]

    with jax.named_scope("exchange_modes"):
        exchanged = []
        for shift in SHIFTS:
            at = (dp + shift) % 4
            both = jnp.stack([lax.dynamic_index_in_dim(v, at, 1, False) for v in (spec, grad)])
            exchanged.append(ring(both, "dp", shift))

    with jax.named_scope("gather_rows"):
        xs = jnp.stack(
            [lax.dynamic_index_in_dim(spec, dp, 1, False)] + [block[0] for block in exchanged], axis=1
        )
        xs_across = flip(xs, "cout", 2)
        xs_beside = flip(jnp.stack([xs, xs_across]), "cout", 1)

    with jax.named_scope("gather_late_grad"):
        late = jnp.stack([block[1] for block in exchanged], axis=1)
        late_line = jnp.stack([late] + [hop(late, shift, 0) for shift in SHIFTS])

    tree = jax.ShapeDtypeStruct((2, 4, 2, 2, 16, 512), jnp.float32)
    keep, send = pl.pallas_call(
        input_terms,
        out_shape=(tree, tree),
        in_specs=[SMEM, SMEM, VMEM, VMEM] + [ANY] * 4,
        out_specs=(VMEM, VMEM),
        scratch_shapes=[pltpu.VMEM((4, 2, 512, 512), jnp.bfloat16), pltpu.SemaphoreType.DMA],
        compiler_params=pltpu.CompilerParams(vmem_limit_bytes=24 * MIB),
        cost_estimate=pl.CostEstimate(flops=1 << 30, bytes_accessed=8 * MIB, transcendentals=0),
        name="input_terms",
    )(blocks, scalars, weight, w_other, *held)
    with jax.named_scope("sum_input"):
        beside = flip(send, "cout", 1)
        across = flip(keep[1] + beside[1], "cout", 2)
        summed = ((keep[0] + beside[0]) + across).astype(jnp.bfloat16)
        own, other = summed[:, :, 0], swap_cores(summed[:, :, 1])
        spectrum_grad = jnp.where(
            core == 0, jnp.concatenate([own, other], axis=0), jnp.concatenate([other, own], axis=0)
        )

    with jax.named_scope("gather_late_grad"):
        late_held = [late_line] + [hop(late_line, shift, 1) for shift in SHIFTS]
    terms = pl.pallas_call(
        weight_terms,
        out_shape=jax.ShapeDtypeStruct((2, 2, 64, 512), jnp.bfloat16),
        in_specs=[SMEM, SMEM] + [ANY] * 11,
        out_specs=VMEM,
        scratch_shapes=[
            pltpu.VMEM((4, 2, 512, 512), jnp.bfloat16),
            pltpu.VMEM((4, 2, 128, 512), jnp.bfloat16),
            pltpu.SemaphoreType.DMA,
        ],
        compiler_params=pltpu.CompilerParams(vmem_limit_bytes=24 * MIB),
        cost_estimate=pl.CostEstimate(flops=1 << 30, bytes_accessed=5 * MIB, transcendentals=0),
        name="weight_terms",
    )(blocks, scalars, *held, *late_held, xs, xs_across, xs_beside)

    with jax.named_scope("spread_weight"):
        finished = jnp.stack([terms[0], swap_cores(terms[1])])
        spread = [ring(finished, "dp", shift) for shift in SHIFTS]
    weight_grad = pl.pallas_call(
        place_modes,
        out_shape=jax.ShapeDtypeStruct(weight.shape, jnp.bfloat16),
        in_specs=[SMEM] + [ANY] * 4,
        out_specs=VMEM,
        scratch_shapes=[pltpu.SemaphoreType.DMA],
        compiler_params=pltpu.CompilerParams(vmem_limit_bytes=8 * MIB),
        cost_estimate=pl.CostEstimate(flops=0, bytes_accessed=2 * MIB, transcendentals=0),
        name="place_modes",
    )(scalars, finished, *spread)
    return (spectrum_grad, weight_grad)


def solution(mesh):
    placed = (
        P(None, None, "cin", "cout"),
        P(None, None, ("cin", "cout"), "dp"),
        P(None, None, ("cout", "cin"), "dp"),
    )
    return jax.shard_map(
        on_device,
        mesh=mesh,
        in_specs=placed,
        out_specs=(P(None, None, ("cin", "cout"), "dp"), P(None, None, "cin", "cout")),
        check_vma=False,
    )
```

```python
import jax
import jax.numpy as jnp
from jax import lax
from jax.experimental import pallas as pl
from jax.experimental.pallas import tpu as pltpu
from jax.sharding import PartitionSpec as P

HEARD = (0, 3, 2, 1)
SHIFTS = (1, 2, 3)
PAIRED = (0, 1, 3, 2)
TREE = (0, 2, 1, 3)
MIB = 1 << 20
ANY = pl.BlockSpec(memory_space=pl.ANY)
SMEM = pl.BlockSpec(memory_space=pltpu.SMEM)
VMEM = pl.BlockSpec(memory_space=pltpu.VMEM)


def ring(value, axis, shift):
    return lax.ppermute(value, axis, [(i, (i + shift) % 4) for i in range(4)])


def flip(value, axis, bits, size=4):
    return lax.ppermute(value, axis, [(i, i ^ bits) for i in range(size)])


def swap_cores(value):
    return flip(value, "cin", 1, 32)


def hop(value, move, stage):
    pairs = []
    for i in range(32):
        y, x, core = i // 8, (i // 2) % 4, i % 2
        if core == stage:
            x = move(x)
        else:
            y = move(y)
        pairs.append((i, (y * 4 + x) * 2 + core))
    return lax.ppermute(value, "cin", pairs)


def after(value, *earlier):
    return lax.optimization_barrier((value, *earlier))[0]


def first_hops(block):
    two = jnp.stack([block, hop(block, lambda at: at ^ 1, 0)])
    return jnp.concatenate([two, hop(two, lambda at: at ^ 3, 0)])


def second_hops(line):
    return [line] + [hop(line, lambda at, shift=shift: (at + shift) % 4, 1) for shift in SHIFTS]


def plane_row(position, second, first, source):
    place = position[1]
    core = place & 1
    along_x, along_y = (place >> 1) & 3, place >> 3
    across = jnp.where(core == 0, along_x ^ PAIRED[first], (along_x + HEARD[second]) & 3)
    down = jnp.where(core == 0, (along_y + HEARD[second]) & 3, along_y ^ PAIRED[first])
    return pl.multiple_of(((down * 4 + across) * 2 + (core ^ source)) * 16, 16)


def tree_row(position, index):
    return pl.multiple_of((position[2] ^ TREE[index]) * 16, 16)


def fetch_plane(position, pieces, source_of, target, sem):
    for second in range(4):
        for first in range(4):
            for source in range(2):
                row = plane_row(position, second, first, source)
                pltpu.make_async_copy(
                    source_of(pieces[second].at[first], source), target(pl.ds(row, 16)), sem
                ).start()


def input_terms(position, w, w_other, *refs):
    pieces, (keep, send, grads, sem) = refs[:4], refs[4:]
    fetch_plane(
        position,
        pieces,
        lambda piece, source: piece.at[source],
        lambda rows: grads.at[:, :, rows, :],
        sem,
    )
    base = (position[1] & 1) * 4
    rows = [pl.ds(tree_row(position, r), 16) for r in range(4)]
    pltpu.make_async_copy(grads, grads, sem).wait()
    for mode in range(4):
        real, imag = (
            jnp.concatenate(
                [block for row in rows for block in (w[base + mode, part, row, :], w_other[mode, part, row, :])],
                axis=0,
            )
            for part in range(2)
        )
        total = jnp.dot(
            jnp.concatenate([real, -imag], axis=0), grads[mode, 0], preferred_element_type=jnp.float32
        ) + jnp.dot(
            jnp.concatenate([imag, real], axis=0), grads[mode, 1], preferred_element_type=jnp.float32
        )
        total = total.reshape(2, 4, 2, 16, 512)
        for part in range(2):
            for r in range(2):
                keep[r, mode, part] = total[part, r]
                send[r, mode, part] = total[part, r + 2]


def weight_terms(position, *refs):
    pieces, late, (x0, x1, x2, out, grads, rows, sem) = refs[:4], refs[4:8], refs[8:]
    mode = position[0]
    fetch_plane(
        position,
        pieces,
        lambda piece, source: piece.at[source, mode],
        lambda place: grads.at[0, :, place, :],
        sem,
    )
    for index, piece in enumerate((x0, x1, x2.at[0], x2.at[1])):
        for source in range(2):
            row = pl.multiple_of(tree_row(position, index) + 64 * source, 16)
            pltpu.make_async_copy(piece.at[source], rows.at[:, :, pl.ds(row, 16), :], sem).start()
    fetch_plane(
        position,
        late,
        lambda piece, source: piece.at[:, source],
        lambda place: grads.at[pl.ds(1, 3), :, place, :],
        sem,
    )
    pltpu.make_async_copy(grads, grads, sem).wait()
    pltpu.make_async_copy(rows, rows, sem).wait()

    total = jnp.zeros((256, 512), jnp.float32)
    contract = (((1,), (1,)), ((), ()))
    for block in range(4):
        real = rows[block, 0]
        imag = rows[block, 1]
        total += lax.dot_general(
            jnp.concatenate([real, -imag], axis=0), grads[block, 0], contract, preferred_element_type=jnp.float32
        )
        total += lax.dot_general(
            jnp.concatenate([imag, real], axis=0), grads[block, 1], contract, preferred_element_type=jnp.float32
        )
    for part in range(2):
        for source in range(2):
            start = part * 128 + source * 64
            out[source, part] = total[start : start + 64].astype(jnp.bfloat16)


def place_modes(position, own, back, far, ahead, out, sem):
    for step, piece in enumerate((own, back, far, ahead)):
        for slot in range(2):
            mode = ((position[1] & 1) ^ slot) * 4 + ((position[0] + HEARD[step]) & 3)
            pltpu.make_async_copy(piece.at[slot], out.at[mode], sem).start()
    pltpu.make_async_copy(out, out, sem).wait()


def on_device(weight, spectrum, out_grad):
    dp, place, cout = lax.axis_index("dp"), lax.axis_index("cin"), lax.axis_index("cout")
    core = place & 1
    position = jnp.stack([dp, place, cout]).astype(jnp.int32)

    def modes_of(value, start, count):
        return lax.dynamic_slice_in_dim(value, start, count, 0)

    mine, theirs = 4 * core, 4 - 4 * core
    with jax.named_scope("swap_modes"):
        swapped = swap_cores(
            jnp.concatenate([modes_of(v, theirs, 4) for v in (weight, spectrum, out_grad)], axis=2)
        )
        spec = jnp.stack([modes_of(spectrum, mine, 4), swapped[:, :, 64:80]])
        grad = jnp.stack([modes_of(out_grad, mine, 4), swapped[:, :, 80:]])

    with jax.named_scope("gather_grad"):
        line = first_hops(grad)
        held = second_hops(line)

    with jax.named_scope("exchange_modes"):
        exchanged = []
        for shift in SHIFTS:
            at = (dp + shift) & 3
            both = jnp.stack([lax.dynamic_index_in_dim(v, at, 1, False) for v in (spec, grad)])
            exchanged.append(ring(both, "dp", shift))

    with jax.named_scope("gather_rows"):
        xs = jnp.stack(
            [lax.dynamic_index_in_dim(spec, dp, 1, False)] + [block[0] for block in exchanged], axis=1
        )
        xs_across = flip(xs, "cout", 2)
        xs_beside = flip(jnp.stack([xs, xs_across]), "cout", 1)

    with jax.named_scope("gather_late_grad"):
        late = jnp.stack([block[1] for block in exchanged])
        late_line = first_hops(late)

    tree = jax.ShapeDtypeStruct((2, 4, 2, 2, 16, 512), jnp.float32)
    keep, send = pl.pallas_call(
        input_terms,
        out_shape=(tree, tree),
        in_specs=[SMEM, VMEM, VMEM] + [ANY] * 4,
        out_specs=(VMEM, VMEM),
        scratch_shapes=[pltpu.VMEM((4, 2, 512, 512), jnp.bfloat16), pltpu.SemaphoreType.DMA],
        compiler_params=pltpu.CompilerParams(vmem_limit_bytes=24 * MIB),
        cost_estimate=pl.CostEstimate(flops=1 << 30, bytes_accessed=8 * MIB, transcendentals=0),
        name="input_terms",
    )(position, weight, swapped, *held)
    with jax.named_scope("sum_input"):
        beside = flip(after(send, xs_across), "cout", 1)
        across = flip(keep[1] + beside[1], "cout", 2)
        summed = ((keep[0] + beside[0]) + across).astype(jnp.bfloat16)
        own, other = summed[:, :, 0], swap_cores(summed[:, :, 1])
        spectrum_grad = jnp.where(
            core == 0, jnp.concatenate([own, other], axis=0), jnp.concatenate([other, own], axis=0)
        )

    with jax.named_scope("gather_late_grad"):
        late_held = second_hops(late_line)
    terms = pl.pallas_call(
        weight_terms,
        out_shape=jax.ShapeDtypeStruct((2, 2, 64, 512), jnp.bfloat16),
        in_specs=[SMEM] + [ANY] * 11,
        out_specs=VMEM,
        scratch_shapes=[
            pltpu.VMEM((4, 2, 512, 512), jnp.bfloat16),
            pltpu.VMEM((4, 2, 128, 512), jnp.bfloat16),
            pltpu.SemaphoreType.DMA,
        ],
        compiler_params=pltpu.CompilerParams(vmem_limit_bytes=24 * MIB),
        cost_estimate=pl.CostEstimate(flops=1 << 30, bytes_accessed=5 * MIB, transcendentals=0),
        name="weight_terms",
    )(position, *held, *late_held, xs, xs_across, xs_beside)

    with jax.named_scope("spread_weight"):
        finished = jnp.stack([terms[0], swap_cores(terms[1])])
        spread = [ring(finished, "dp", shift) for shift in SHIFTS]
    weight_grad = pl.pallas_call(
        place_modes,
        out_shape=jax.ShapeDtypeStruct(weight.shape, jnp.bfloat16),
        in_specs=[SMEM] + [ANY] * 4,
        out_specs=VMEM,
        scratch_shapes=[pltpu.SemaphoreType.DMA],
        compiler_params=pltpu.CompilerParams(vmem_limit_bytes=8 * MIB),
        cost_estimate=pl.CostEstimate(flops=0, bytes_accessed=2 * MIB, transcendentals=0),
        name="place_modes",
    )(position, finished, *spread)
    return (spectrum_grad, weight_grad)


def solution(mesh):
    placed = (
        P(None, None, "cin", "cout"),
        P(None, None, ("cin", "cout"), "dp"),
        P(None, None, ("cout", "cin"), "dp"),
    )
    return jax.shard_map(
        on_device,
        mesh=mesh,
        in_specs=placed,
        out_specs=(P(None, None, ("cin", "cout"), "dp"), P(None, None, "cin", "cout")),
        check_vma=False,
    )
```

```python
import jax
import jax.numpy as jnp
from jax import lax
from jax.experimental import pallas as pl
from jax.experimental.pallas import tpu as pltpu
from jax.sharding import PartitionSpec as P

HEARD = (0, 3, 2, 1)
SHIFTS = (1, 2, 3)
PAIRED = (0, 1, 3, 2)
TREE = (0, 2, 1, 3)
MIB = 1 << 20
ANY = pl.BlockSpec(memory_space=pl.ANY)
SMEM = pl.BlockSpec(memory_space=pltpu.SMEM)
VMEM = pl.BlockSpec(memory_space=pltpu.VMEM)


def ring(value, axis, shift):
    return lax.ppermute(value, axis, [(i, (i + shift) % 4) for i in range(4)])


def flip(value, axis, bits, size=4):
    return lax.ppermute(value, axis, [(i, i ^ bits) for i in range(size)])


def swap_cores(value):
    return flip(value, "cin", 1, 32)


def hop(value, move, stage):
    pairs = []
    for i in range(32):
        y, x, core = i // 8, (i // 2) % 4, i % 2
        if core == stage:
            x = move(x)
        else:
            y = move(y)
        pairs.append((i, (y * 4 + x) * 2 + core))
    return lax.ppermute(value, "cin", pairs)


def after(value, *earlier):
    return lax.optimization_barrier((value, *earlier))[0]


def first_hops(block):
    two = jnp.stack([block, hop(block, lambda at: at ^ 1, 0)])
    return jnp.concatenate([two, hop(two, lambda at: at ^ 3, 0)])


def second_hops(line):
    return [line] + [hop(line, lambda at, shift=shift: (at + shift) % 4, 1) for shift in SHIFTS]


def plane_row(position, second, first, source):
    place = position[1]
    core = place & 1
    along_x, along_y = (place >> 1) & 3, place >> 3
    across = jnp.where(core == 0, along_x ^ PAIRED[first], (along_x + HEARD[second]) & 3)
    down = jnp.where(core == 0, (along_y + HEARD[second]) & 3, along_y ^ PAIRED[first])
    return pl.multiple_of(((down * 4 + across) * 2 + (core ^ source)) * 16, 16)


def tree_row(position, index):
    return pl.multiple_of((position[2] ^ TREE[index]) * 16, 16)


def fetch_plane(position, pieces, source_of, target, sem):
    for second in range(4):
        for first in range(4):
            for source in range(2):
                row = plane_row(position, second, first, source)
                pltpu.make_async_copy(
                    source_of(pieces[second].at[first], source), target(pl.ds(row, 16)), sem
                ).start()


def input_terms(position, w, w_other, *refs):
    pieces, (keep, send, grads, sem) = refs[:4], refs[4:]
    fetch_plane(
        position,
        pieces,
        lambda piece, source: piece.at[source],
        lambda rows: grads.at[:, :, rows, :],
        sem,
    )
    base = (position[1] & 1) * 4
    rows = [pl.ds(tree_row(position, r), 16) for r in range(4)]
    pltpu.make_async_copy(grads, grads, sem).wait()
    for mode in range(4):
        real, imag = (
            jnp.concatenate(
                [block for row in rows for block in (w[base + mode, part, row, :], w_other[mode, part, row, :])],
                axis=0,
            )
            for part in range(2)
        )
        total = jnp.dot(
            jnp.concatenate([real, -imag], axis=0), grads[mode, 0], preferred_element_type=jnp.float32
        ) + jnp.dot(
            jnp.concatenate([imag, real], axis=0), grads[mode, 1], preferred_element_type=jnp.float32
        )
        total = total.reshape(2, 4, 2, 16, 512)
        for part in range(2):
            for r in range(2):
                keep[r, mode, part] = total[part, r]
                send[r, mode, part] = total[part, r + 2]


def weight_terms(position, *refs):
    pieces, late, (x0, x1, x2, here, there, grads, rows, sem) = refs[:4], refs[4:8], refs[8:]
    mode = position[0]
    fetch_plane(
        position,
        pieces,
        lambda piece, source: piece.at[source, mode],
        lambda place: grads.at[0, :, place, :],
        sem,
    )
    for index, piece in enumerate((x0, x1, x2.at[0], x2.at[1])):
        for source in range(2):
            row = pl.multiple_of(tree_row(position, index) + 64 * source, 16)
            pltpu.make_async_copy(piece.at[source], rows.at[:, :, pl.ds(row, 16), :], sem).start()
    fetch_plane(
        position,
        late,
        lambda piece, source: piece.at[:, source],
        lambda place: grads.at[pl.ds(1, 3), :, place, :],
        sem,
    )
    pltpu.make_async_copy(grads, grads, sem).wait()
    pltpu.make_async_copy(rows, rows, sem).wait()

    total = jnp.zeros((256, 512), jnp.float32)
    contract = (((1,), (1,)), ((), ()))
    for block in range(4):
        real = rows[block, 0]
        imag = rows[block, 1]
        total += lax.dot_general(
            jnp.concatenate([real, -imag], axis=0), grads[block, 0], contract, preferred_element_type=jnp.float32
        )
        total += lax.dot_general(
            jnp.concatenate([imag, real], axis=0), grads[block, 1], contract, preferred_element_type=jnp.float32
        )
    for part in range(2):
        for source, out in enumerate((here, there)):
            start = part * 128 + source * 64
            out[part] = total[start : start + 64].astype(jnp.bfloat16)


def place_modes(position, *refs):
    pieces, (out, sem) = refs[:8], refs[8:]
    for step in range(4):
        for slot in range(2):
            mode = ((position[1] & 1) ^ slot) * 4 + ((position[0] + HEARD[step]) & 3)
            pltpu.make_async_copy(pieces[2 * step + slot], out.at[mode], sem).start()
    pltpu.make_async_copy(out, out, sem).wait()


def on_device(weight, spectrum, out_grad):
    dp, place, cout = lax.axis_index("dp"), lax.axis_index("cin"), lax.axis_index("cout")
    core = place & 1
    position = jnp.stack([dp, place, cout]).astype(jnp.int32)

    def modes_of(value, start, count):
        return lax.dynamic_slice_in_dim(value, start, count, 0)

    mine, theirs = 4 * core, 4 - 4 * core
    with jax.named_scope("swap_modes"):
        swapped = swap_cores(
            jnp.concatenate([modes_of(v, theirs, 4) for v in (weight, spectrum, out_grad)], axis=2)
        )
        spec = jnp.stack([modes_of(spectrum, mine, 4), swapped[:, :, 64:80]])
        grad = jnp.stack([modes_of(out_grad, mine, 4), swapped[:, :, 80:]])

    with jax.named_scope("gather_grad"):
        line = first_hops(grad)
        held = second_hops(line)

    with jax.named_scope("exchange_modes"):
        exchanged = []
        for shift in SHIFTS:
            at = (dp + shift) & 3
            both = jnp.stack([lax.dynamic_index_in_dim(v, at, 1, False) for v in (spec, grad)])
            exchanged.append(ring(both, "dp", shift))

    with jax.named_scope("gather_rows"):
        xs = jnp.stack(
            [lax.dynamic_index_in_dim(spec, dp, 1, False)] + [block[0] for block in exchanged], axis=1
        )
        xs_across = flip(xs, "cout", 2)
        xs_beside = flip(jnp.stack([xs, xs_across]), "cout", 1)

    with jax.named_scope("gather_late_grad"):
        late = jnp.stack([block[1] for block in exchanged])
        late_line = first_hops(late)

    tree = jax.ShapeDtypeStruct((2, 4, 2, 2, 16, 512), jnp.float32)
    keep, send = pl.pallas_call(
        input_terms,
        out_shape=(tree, tree),
        in_specs=[SMEM, VMEM, VMEM] + [ANY] * 4,
        out_specs=(VMEM, VMEM),
        scratch_shapes=[pltpu.VMEM((4, 2, 512, 512), jnp.bfloat16), pltpu.SemaphoreType.DMA],
        compiler_params=pltpu.CompilerParams(vmem_limit_bytes=24 * MIB),
        cost_estimate=pl.CostEstimate(flops=1 << 30, bytes_accessed=8 * MIB, transcendentals=0),
        name="input_terms",
    )(position, weight, swapped, *held)
    with jax.named_scope("sum_input"):
        beside = flip(after(send, xs_across), "cout", 1)
        across = flip(keep[1] + beside[1], "cout", 2)
        summed = ((keep[0] + beside[0]) + across).astype(jnp.bfloat16)
        own, other = summed[:, :, 0], swap_cores(summed[:, :, 1])
        spectrum_grad = jnp.where(
            core == 0, jnp.concatenate([own, other], axis=0), jnp.concatenate([other, own], axis=0)
        )

    with jax.named_scope("gather_late_grad"):
        late_held = second_hops(late_line)
    here, there = pl.pallas_call(
        weight_terms,
        out_shape=[jax.ShapeDtypeStruct((2, 64, 512), jnp.bfloat16)] * 2,
        in_specs=[SMEM] + [ANY] * 11,
        out_specs=[VMEM] * 2,
        scratch_shapes=[
            pltpu.VMEM((4, 2, 512, 512), jnp.bfloat16),
            pltpu.VMEM((4, 2, 128, 512), jnp.bfloat16),
            pltpu.SemaphoreType.DMA,
        ],
        compiler_params=pltpu.CompilerParams(vmem_limit_bytes=24 * MIB),
        cost_estimate=pl.CostEstimate(flops=1 << 30, bytes_accessed=5 * MIB, transcendentals=0),
        name="weight_terms",
    )(position, *held, *late_held, xs, xs_across, xs_beside)

    with jax.named_scope("spread_weight"):
        back_0, ahead_0 = ring(here, "dp", 1), ring(here, "dp", 3)
        other = swap_cores(there)
        back_1, ahead_1 = ring(other, "dp", 1), ring(other, "dp", 3)
        far_0, far_1 = ring(back_0, "dp", 1), ring(ahead_1, "dp", 3)
    weight_grad = pl.pallas_call(
        place_modes,
        out_shape=jax.ShapeDtypeStruct(weight.shape, jnp.bfloat16),
        in_specs=[SMEM] + [ANY] * 8,
        out_specs=VMEM,
        scratch_shapes=[pltpu.SemaphoreType.DMA],
        compiler_params=pltpu.CompilerParams(vmem_limit_bytes=8 * MIB),
        cost_estimate=pl.CostEstimate(flops=0, bytes_accessed=2 * MIB, transcendentals=0),
        name="place_modes",
    )(position, here, other, back_0, back_1, far_0, far_1, ahead_0, ahead_1)
    return (spectrum_grad, weight_grad)


def solution(mesh):
    placed = (
        P(None, None, "cin", "cout"),
        P(None, None, ("cin", "cout"), "dp"),
        P(None, None, ("cout", "cin"), "dp"),
    )
    return jax.shard_map(
        on_device,
        mesh=mesh,
        in_specs=placed,
        out_specs=(P(None, None, ("cin", "cout"), "dp"), P(None, None, "cin", "cout")),
        check_vma=False,
    )
```

```python
import functools

import jax
import jax.numpy as jnp
from jax import lax
from jax.experimental import pallas as pl
from jax.experimental.pallas import tpu as pltpu
from jax.sharding import PartitionSpec as P

HEARD = (0, 3, 2, 1)
SHIFTS = (1, 2, 3)
ARRIVAL = (0, 3, 1, 2)
PAIRED = (0, 1, 3, 2)
TREE = (0, 2, 1, 3)
MIB = 1 << 20
ANY = pl.BlockSpec(memory_space=pl.ANY)
SMEM = pl.BlockSpec(memory_space=pltpu.SMEM)
VMEM = pl.BlockSpec(memory_space=pltpu.VMEM)


def ring(value, axis, shift):
    return lax.ppermute(value, axis, [(i, (i + shift) % 4) for i in range(4)])


def flip(value, axis, bits, size=4):
    return lax.ppermute(value, axis, [(i, i ^ bits) for i in range(size)])


def swap_cores(value):
    return flip(value, "cin", 1, 32)


def hop(value, move, stage):
    pairs = []
    for i in range(32):
        y, x, core = i // 8, (i // 2) % 4, i % 2
        if core == stage:
            x = move(x)
        else:
            y = move(y)
        pairs.append((i, (y * 4 + x) * 2 + core))
    return lax.ppermute(value, "cin", pairs)


def after(value, *earlier):
    return lax.optimization_barrier((value, *earlier))[0]


def first_hops(block):
    two = jnp.stack([block, hop(block, lambda at: at ^ 1, 0)])
    return jnp.concatenate([two, hop(two, lambda at: at ^ 3, 0)])


def second_hops(line):
    return [line] + [hop(line, lambda at, shift=shift: (at + shift) % 4, 1) for shift in SHIFTS]


def plane_row(position, second, first, source):
    place = position[1]
    core = place & 1
    along_x, along_y = (place >> 1) & 3, place >> 3
    across = jnp.where(core == 0, along_x ^ PAIRED[first], (along_x + HEARD[second]) & 3)
    down = jnp.where(core == 0, (along_y + HEARD[second]) & 3, along_y ^ PAIRED[first])
    return pl.multiple_of(((down * 4 + across) * 2 + (core ^ source)) * 16, 16)


def tree_row(position, index):
    return pl.multiple_of((position[2] ^ TREE[index]) * 16, 16)


def fetch_plane(position, pieces, source_of, target, sem):
    for second in range(4):
        for first in range(4):
            for source in range(2):
                row = plane_row(position, second, first, source)
                pltpu.make_async_copy(
                    source_of(pieces[second].at[first], source), target(pl.ds(row, 16)), sem
                ).start()


def input_terms(position, w, w_other, *refs):
    pieces, (keep, send, grads, sem) = refs[:4], refs[4:]
    fetch_plane(
        position,
        pieces,
        lambda piece, source: piece.at[source],
        lambda rows: grads.at[:, :, rows, :],
        sem,
    )
    base = (position[1] & 1) * 4
    rows = [pl.ds(tree_row(position, r), 16) for r in range(4)]
    pltpu.make_async_copy(grads, grads, sem).wait()
    for mode in range(4):
        real, imag = (
            jnp.concatenate(
                [block for row in rows for block in (w[base + mode, part, row, :], w_other[mode, part, row, :])],
                axis=0,
            )
            for part in range(2)
        )
        total = jnp.dot(
            jnp.concatenate([real, -imag], axis=0), grads[mode, 0], preferred_element_type=jnp.float32
        ) + jnp.dot(
            jnp.concatenate([imag, real], axis=0), grads[mode, 1], preferred_element_type=jnp.float32
        )
        total = total.reshape(2, 4, 2, 16, 512)
        for part in range(2):
            for r in range(2):
                keep[r, mode, part] = total[part, r]
                send[r, mode, part] = total[part, r + 2]


def weight_terms(position, *refs):
    pieces, late, (x0, x1, x2, here, there, grads, rows, sems) = refs[:4], refs[4:8], refs[8:]
    mode = position[0]
    fetch_plane(
        position,
        pieces,
        lambda piece, source: piece.at[source, mode],
        lambda place: grads.at[0, :, place, :],
        sems.at[0],
    )
    for index, piece in enumerate((x0, x1, x2.at[0], x2.at[1])):
        for source in range(2):
            row = pl.multiple_of(tree_row(position, index) + 64 * source, 16)
            pltpu.make_async_copy(piece.at[source], rows.at[:, :, pl.ds(row, 16), :], sems.at[0]).start()
    fetch_plane(
        position,
        late,
        lambda piece, source: piece.at[:, source],
        lambda place: grads.at[pl.ds(1, 3), :, place, :],
        sems.at[1],
    )
    pltpu.make_async_copy(grads.at[0], grads.at[0], sems.at[0]).wait()
    pltpu.make_async_copy(rows, rows, sems.at[0]).wait()

    total = jnp.zeros((256, 512), jnp.float32)
    contract = (((1,), (1,)), ((), ()))
    for block in range(4):
        if block == 1:
            pltpu.make_async_copy(grads.at[pl.ds(1, 3)], grads.at[pl.ds(1, 3)], sems.at[1]).wait()
        real = rows[block, 0]
        imag = rows[block, 1]
        total += lax.dot_general(
            jnp.concatenate([real, -imag], axis=0), grads[block, 0], contract, preferred_element_type=jnp.float32
        )
        total += lax.dot_general(
            jnp.concatenate([imag, real], axis=0), grads[block, 1], contract, preferred_element_type=jnp.float32
        )
    for part in range(2):
        for source, out in enumerate((here, there)):
            start = part * 128 + source * 64
            out[part] = total[start : start + 64].astype(jnp.bfloat16)


def place_modes(first, position, *refs):
    pieces, (out, staged, read, written) = refs[:-4], refs[-4:]
    reads = [
        pltpu.make_async_copy(piece, staged.at[index], read.at[index]) for index, piece in enumerate(pieces)
    ]
    for copy in reads:
        copy.start()
    for index, copy in enumerate(reads):
        slot, step = (first + index) % 2, (first + index) // 2
        mode = ((position[1] & 1) ^ slot) * 4 + ((position[0] + ARRIVAL[step]) & 3)
        copy.wait()
        pltpu.make_async_copy(staged.at[index], out.at[mode], written).start()
    pltpu.make_async_copy(staged, staged, written).wait()


def place_last(position, piece, placed, out, staged, read, written):
    del placed
    place_modes(7, position, piece, out, staged, read, written)


def place_call(body, name, pieces, position, placed=None):
    held = [] if placed is None else [placed]
    return pl.pallas_call(
        body,
        out_shape=jax.ShapeDtypeStruct((8, 2, 64, 512), jnp.bfloat16),
        in_specs=[SMEM] + [ANY] * (len(pieces) + len(held)),
        out_specs=ANY,
        input_output_aliases={1 + len(pieces): 0} if held else {},
        scratch_shapes=[
            pltpu.VMEM((len(pieces), 2, 64, 512), jnp.bfloat16),
            pltpu.SemaphoreType.DMA((len(pieces),)),
            pltpu.SemaphoreType.DMA,
        ],
        compiler_params=pltpu.CompilerParams(vmem_limit_bytes=8 * MIB),
        cost_estimate=pl.CostEstimate(flops=0, bytes_accessed=2 * MIB, transcendentals=0),
        name=name,
    )(position, *pieces, *held)


def on_device(weight, spectrum, out_grad):
    dp, place, cout = lax.axis_index("dp"), lax.axis_index("cin"), lax.axis_index("cout")
    core = place & 1
    position = jnp.stack([dp, place, cout]).astype(jnp.int32)

    def modes_of(value, start, count):
        return lax.dynamic_slice_in_dim(value, start, count, 0)

    mine, theirs = 4 * core, 4 - 4 * core
    with jax.named_scope("swap_modes"):
        swapped = swap_cores(
            jnp.concatenate([modes_of(v, theirs, 4) for v in (weight, spectrum, out_grad)], axis=2)
        )
        spec = jnp.stack([modes_of(spectrum, mine, 4), swapped[:, :, 64:80]])
        grad = jnp.stack([modes_of(out_grad, mine, 4), swapped[:, :, 80:]])

    with jax.named_scope("gather_grad"):
        line = first_hops(grad)
        held = second_hops(line)

    with jax.named_scope("exchange_modes"):
        exchanged = []
        for shift in SHIFTS:
            at = (dp + shift) & 3
            both = jnp.stack([lax.dynamic_index_in_dim(v, at, 1, False) for v in (spec, grad)])
            exchanged.append(ring(both, "dp", shift))

    with jax.named_scope("gather_rows"):
        xs = jnp.stack(
            [lax.dynamic_index_in_dim(spec, dp, 1, False)] + [block[0] for block in exchanged], axis=1
        )
        xs_across = flip(xs, "cout", 2)
        xs_beside = flip(jnp.stack([xs, xs_across]), "cout", 1)

    with jax.named_scope("gather_late_grad"):
        late = jnp.stack([block[1] for block in exchanged])
        late_line = first_hops(late)

    tree = jax.ShapeDtypeStruct((2, 4, 2, 2, 16, 512), jnp.float32)
    keep, send = pl.pallas_call(
        input_terms,
        out_shape=(tree, tree),
        in_specs=[SMEM, VMEM, VMEM] + [ANY] * 4,
        out_specs=(VMEM, VMEM),
        scratch_shapes=[pltpu.VMEM((4, 2, 512, 512), jnp.bfloat16), pltpu.SemaphoreType.DMA],
        compiler_params=pltpu.CompilerParams(vmem_limit_bytes=24 * MIB),
        cost_estimate=pl.CostEstimate(flops=1 << 30, bytes_accessed=8 * MIB, transcendentals=0),
        name="input_terms",
    )(position, weight, swapped, *held)
    with jax.named_scope("sum_input"):
        beside = flip(after(send, xs_across), "cout", 1)
        across = flip(keep[1] + beside[1], "cout", 2)
        summed = ((keep[0] + beside[0]) + across).astype(jnp.bfloat16)
        own, other = summed[:, :, 0], swap_cores(summed[:, :, 1])
        spectrum_grad = jnp.where(
            core == 0, jnp.concatenate([own, other], axis=0), jnp.concatenate([other, own], axis=0)
        )

    with jax.named_scope("gather_late_grad"):
        late_held = second_hops(late_line)
    here, there = pl.pallas_call(
        weight_terms,
        out_shape=[jax.ShapeDtypeStruct((2, 64, 512), jnp.bfloat16)] * 2,
        in_specs=[SMEM] + [ANY] * 11,
        out_specs=[VMEM] * 2,
        scratch_shapes=[
            pltpu.VMEM((4, 2, 512, 512), jnp.bfloat16),
            pltpu.VMEM((4, 2, 128, 512), jnp.bfloat16),
            pltpu.SemaphoreType.DMA((2,)),
        ],
        compiler_params=pltpu.CompilerParams(vmem_limit_bytes=24 * MIB),
        cost_estimate=pl.CostEstimate(flops=1 << 30, bytes_accessed=5 * MIB, transcendentals=0),
        name="weight_terms",
    )(position, *held, *late_held, xs, xs_across, xs_beside)

    with jax.named_scope("spread_weight"):
        back_0, ahead_0 = ring(here, "dp", 1), ring(here, "dp", 3)
        other = swap_cores(there)
        back_1, ahead_1 = ring(other, "dp", 1), ring(other, "dp", 3)
        far_0, far_1 = ring(back_0, "dp", 1), ring(ahead_1, "dp", 3)
    placed = place_call(
        functools.partial(place_modes, 0),
        "place_modes",
        [here, other, back_0, back_1, ahead_0, ahead_1, far_0],
        position,
    )
    weight_grad = place_call(place_last, "place_last", [far_1], position, placed)
    return (spectrum_grad, weight_grad)


def solution(mesh):
    placed = (
        P(None, None, "cin", "cout"),
        P(None, None, ("cin", "cout"), "dp"),
        P(None, None, ("cout", "cin"), "dp"),
    )
    return jax.shard_map(
        on_device,
        mesh=mesh,
        in_specs=placed,
        out_specs=(P(None, None, ("cin", "cout"), "dp"), P(None, None, "cin", "cout")),
        check_vma=False,
    )
```

```python
import functools

import jax
import jax.numpy as jnp
from jax import lax
from jax.experimental import pallas as pl
from jax.experimental.pallas import tpu as pltpu
from jax.sharding import PartitionSpec as P

HEARD = (0, 3, 2, 1)
SHIFTS = (1, 2, 3)
ARRIVAL = (0, 3, 1, 2)
PAIRED = (0, 1, 3, 2)
TREE = (0, 2, 1, 3)
MIB = 1 << 20
ANY = pl.BlockSpec(memory_space=pl.ANY)
SMEM = pl.BlockSpec(memory_space=pltpu.SMEM)
VMEM = pl.BlockSpec(memory_space=pltpu.VMEM)


def ring(value, axis, shift):
    return lax.ppermute(value, axis, [(i, (i + shift) % 4) for i in range(4)])


def flip(value, axis, bits, size=4):
    return lax.ppermute(value, axis, [(i, i ^ bits) for i in range(size)])


def swap_cores(value):
    return flip(value, "cin", 1, 32)


def hop(value, move, stage):
    pairs = []
    for i in range(32):
        y, x, core = i // 8, (i // 2) % 4, i % 2
        if core == stage:
            x = move(x)
        else:
            y = move(y)
        pairs.append((i, (y * 4 + x) * 2 + core))
    return lax.ppermute(value, "cin", pairs)


def after(value, *earlier):
    return lax.optimization_barrier((value, *earlier))[0]


def first_hops(block):
    two = jnp.stack([block, hop(block, lambda at: at ^ 1, 0)])
    return jnp.concatenate([two, hop(two, lambda at: at ^ 3, 0)])


def second_hops(line):
    return [line] + [hop(line, lambda at, shift=shift: (at + shift) % 4, 1) for shift in SHIFTS]


def plane_row(position, second, first, source):
    place = position[1]
    core = place & 1
    along_x, along_y = (place >> 1) & 3, place >> 3
    across = jnp.where(core == 0, along_x ^ PAIRED[first], (along_x + HEARD[second]) & 3)
    down = jnp.where(core == 0, (along_y + HEARD[second]) & 3, along_y ^ PAIRED[first])
    return pl.multiple_of(((down * 4 + across) * 2 + (core ^ source)) * 16, 16)


def tree_row(position, index):
    return pl.multiple_of((position[2] ^ TREE[index]) * 16, 16)


def fetch_plane(position, pieces, source_of, target, sem):
    for second in range(4):
        for first in range(4):
            for source in range(2):
                row = plane_row(position, second, first, source)
                pltpu.make_async_copy(
                    source_of(pieces[second].at[first], source), target(pl.ds(row, 16)), sem
                ).start()


def input_terms(position, w, w_other, *refs):
    pieces, (keep, send, grads, sems) = refs[:4], refs[4:]
    for half in range(2):
        modes = pl.ds(2 * half, 2)
        fetch_plane(
            position,
            pieces,
            lambda piece, source, modes=modes: piece.at[source, modes],
            lambda rows, modes=modes: grads.at[modes, :, rows, :],
            sems.at[half],
        )
    base = (position[1] & 1) * 4
    rows = [pl.ds(tree_row(position, r), 16) for r in range(4)]
    for mode in range(4):
        if mode % 2 == 0:
            arrived = grads.at[pl.ds(mode, 2)]
            pltpu.make_async_copy(arrived, arrived, sems.at[mode // 2]).wait()
        real, imag = (
            jnp.concatenate(
                [block for row in rows for block in (w[base + mode, part, row, :], w_other[mode, part, row, :])],
                axis=0,
            )
            for part in range(2)
        )
        total = jnp.dot(
            jnp.concatenate([real, -imag], axis=0), grads[mode, 0], preferred_element_type=jnp.float32
        ) + jnp.dot(
            jnp.concatenate([imag, real], axis=0), grads[mode, 1], preferred_element_type=jnp.float32
        )
        total = total.reshape(2, 4, 2, 16, 512)
        for part in range(2):
            for r in range(2):
                keep[r, mode, part] = total[part, r]
                send[r, mode, part] = total[part, r + 2]


def weight_terms(position, *refs):
    pieces, late, (x0, x1, x2, here, there, grads, rows, sems) = refs[:4], refs[4:8], refs[8:]
    mode = position[0]
    fetch_plane(
        position,
        pieces,
        lambda piece, source: piece.at[source, mode],
        lambda place: grads.at[0, :, place, :],
        sems.at[0],
    )
    for index, piece in enumerate((x0, x1, x2.at[0], x2.at[1])):
        for source in range(2):
            row = pl.multiple_of(tree_row(position, index) + 64 * source, 16)
            pltpu.make_async_copy(piece.at[source], rows.at[:, :, pl.ds(row, 16), :], sems.at[0]).start()
    fetch_plane(
        position,
        late,
        lambda piece, source: piece.at[:, source],
        lambda place: grads.at[pl.ds(1, 3), :, place, :],
        sems.at[1],
    )
    pltpu.make_async_copy(grads.at[0], grads.at[0], sems.at[0]).wait()
    pltpu.make_async_copy(rows, rows, sems.at[0]).wait()

    total = jnp.zeros((256, 512), jnp.float32)
    contract = (((1,), (1,)), ((), ()))
    for block in range(4):
        if block == 1:
            pltpu.make_async_copy(grads.at[pl.ds(1, 3)], grads.at[pl.ds(1, 3)], sems.at[1]).wait()
        real = rows[block, 0]
        imag = rows[block, 1]
        total += lax.dot_general(
            jnp.concatenate([real, -imag], axis=0), grads[block, 0], contract, preferred_element_type=jnp.float32
        )
        total += lax.dot_general(
            jnp.concatenate([imag, real], axis=0), grads[block, 1], contract, preferred_element_type=jnp.float32
        )
    for part in range(2):
        for source, out in enumerate((here, there)):
            start = part * 128 + source * 64
            out[part] = total[start : start + 64].astype(jnp.bfloat16)


def place_modes(first, position, *refs):
    pieces, (out, staged, read, written) = refs[:-4], refs[-4:]
    reads = [
        pltpu.make_async_copy(piece, staged.at[index], read.at[index]) for index, piece in enumerate(pieces)
    ]
    for copy in reads:
        copy.start()
    for index, copy in enumerate(reads):
        slot, step = (first + index) % 2, (first + index) // 2
        mode = ((position[1] & 1) ^ slot) * 4 + ((position[0] + ARRIVAL[step]) & 3)
        copy.wait()
        pltpu.make_async_copy(staged.at[index], out.at[mode], written).start()
    pltpu.make_async_copy(staged, staged, written).wait()


def place_last(position, piece, placed, out, staged, read, written):
    del placed
    place_modes(7, position, piece, out, staged, read, written)


def place_call(body, name, pieces, position, placed=None):
    held = [] if placed is None else [placed]
    return pl.pallas_call(
        body,
        out_shape=jax.ShapeDtypeStruct((8, 2, 64, 512), jnp.bfloat16),
        in_specs=[SMEM] + [ANY] * (len(pieces) + len(held)),
        out_specs=ANY,
        input_output_aliases={1 + len(pieces): 0} if held else {},
        scratch_shapes=[
            pltpu.VMEM((len(pieces), 2, 64, 512), jnp.bfloat16),
            pltpu.SemaphoreType.DMA((len(pieces),)),
            pltpu.SemaphoreType.DMA,
        ],
        compiler_params=pltpu.CompilerParams(vmem_limit_bytes=8 * MIB),
        cost_estimate=pl.CostEstimate(flops=0, bytes_accessed=2 * MIB, transcendentals=0),
        name=name,
    )(position, *pieces, *held)


def on_device(weight, spectrum, out_grad):
    dp, place, cout = lax.axis_index("dp"), lax.axis_index("cin"), lax.axis_index("cout")
    core = place & 1
    position = jnp.stack([dp, place, cout]).astype(jnp.int32)

    def modes_of(value, start, count):
        return lax.dynamic_slice_in_dim(value, start, count, 0)

    mine, theirs = 4 * core, 4 - 4 * core
    with jax.named_scope("swap_modes"):
        swapped = swap_cores(
            jnp.concatenate([modes_of(v, theirs, 4) for v in (weight, spectrum, out_grad)], axis=2)
        )
        spec = jnp.stack([modes_of(spectrum, mine, 4), swapped[:, :, 64:80]])
        grad = jnp.stack([modes_of(out_grad, mine, 4), swapped[:, :, 80:]])

    with jax.named_scope("gather_grad"):
        line = first_hops(grad)
        held = second_hops(line)

    with jax.named_scope("exchange_modes"):
        exchanged = []
        for shift in SHIFTS:
            at = (dp + shift) & 3
            both = jnp.stack([lax.dynamic_index_in_dim(v, at, 1, False) for v in (spec, grad)])
            exchanged.append(ring(both, "dp", shift))

    with jax.named_scope("gather_rows"):
        xs = jnp.stack(
            [lax.dynamic_index_in_dim(spec, dp, 1, False)] + [block[0] for block in exchanged], axis=1
        )
        xs_across = flip(xs, "cout", 2)
        xs_beside = flip(jnp.stack([xs, xs_across]), "cout", 1)

    with jax.named_scope("gather_late_grad"):
        late = jnp.stack([block[1] for block in exchanged])
        late_line = first_hops(late)

    tree = jax.ShapeDtypeStruct((2, 4, 2, 2, 16, 512), jnp.float32)
    keep, send = pl.pallas_call(
        input_terms,
        out_shape=(tree, tree),
        in_specs=[SMEM, VMEM, VMEM] + [ANY] * 4,
        out_specs=(VMEM, VMEM),
        scratch_shapes=[pltpu.VMEM((4, 2, 512, 512), jnp.bfloat16), pltpu.SemaphoreType.DMA((2,))],
        compiler_params=pltpu.CompilerParams(vmem_limit_bytes=24 * MIB),
        cost_estimate=pl.CostEstimate(flops=1 << 30, bytes_accessed=8 * MIB, transcendentals=0),
        name="input_terms",
    )(position, weight, swapped, *held)
    with jax.named_scope("sum_input"):
        beside = flip(after(send, xs_across), "cout", 1)
        across = flip(keep[1] + beside[1], "cout", 2)
        summed = ((keep[0] + beside[0]) + across).astype(jnp.bfloat16)
        own, other = summed[:, :, 0], swap_cores(summed[:, :, 1])
        spectrum_grad = jnp.where(
            core == 0, jnp.concatenate([own, other], axis=0), jnp.concatenate([other, own], axis=0)
        )

    with jax.named_scope("gather_late_grad"):
        late_held = second_hops(late_line)
    here, there = pl.pallas_call(
        weight_terms,
        out_shape=[jax.ShapeDtypeStruct((2, 64, 512), jnp.bfloat16)] * 2,
        in_specs=[SMEM] + [ANY] * 11,
        out_specs=[VMEM] * 2,
        scratch_shapes=[
            pltpu.VMEM((4, 2, 512, 512), jnp.bfloat16),
            pltpu.VMEM((4, 2, 128, 512), jnp.bfloat16),
            pltpu.SemaphoreType.DMA((2,)),
        ],
        compiler_params=pltpu.CompilerParams(vmem_limit_bytes=24 * MIB),
        cost_estimate=pl.CostEstimate(flops=1 << 30, bytes_accessed=5 * MIB, transcendentals=0),
        name="weight_terms",
    )(position, *held, *late_held, xs, xs_across, xs_beside)

    with jax.named_scope("spread_weight"):
        back_0, ahead_0 = ring(here, "dp", 1), ring(here, "dp", 3)
        other = swap_cores(there)
        back_1, ahead_1 = ring(other, "dp", 1), ring(other, "dp", 3)
        far_0, far_1 = ring(back_0, "dp", 1), ring(ahead_1, "dp", 3)
    placed = place_call(
        functools.partial(place_modes, 0),
        "place_modes",
        [here, other, back_0, back_1, ahead_0, ahead_1, far_0],
        position,
    )
    weight_grad = place_call(place_last, "place_last", [far_1], position, placed)
    return (spectrum_grad, weight_grad)


def solution(mesh):
    placed = (
        P(None, None, "cin", "cout"),
        P(None, None, ("cin", "cout"), "dp"),
        P(None, None, ("cout", "cin"), "dp"),
    )
    return jax.shard_map(
        on_device,
        mesh=mesh,
        in_specs=placed,
        out_specs=(P(None, None, ("cin", "cout"), "dp"), P(None, None, "cin", "cout")),
        check_vma=False,
    )
```

```python
import functools

import jax
import jax.numpy as jnp
from jax import lax
from jax.experimental import pallas as pl
from jax.experimental.pallas import tpu as pltpu
from jax.sharding import PartitionSpec as P

HEARD = (0, 3, 2, 1)
SHIFTS = (1, 2, 3)
ARRIVAL = (0, 3, 1, 2)
PAIRED = (0, 1, 3, 2)
TREE = (0, 2, 1, 3)
MIB = 1 << 20
ANY = pl.BlockSpec(memory_space=pl.ANY)
SMEM = pl.BlockSpec(memory_space=pltpu.SMEM)
VMEM = pl.BlockSpec(memory_space=pltpu.VMEM)


def ring(value, axis, shift):
    return lax.ppermute(value, axis, [(i, (i + shift) % 4) for i in range(4)])


def flip(value, axis, bits, size=4):
    return lax.ppermute(value, axis, [(i, i ^ bits) for i in range(size)])


def swap_cores(value):
    return flip(value, "cin", 1, 32)


def hop(value, move, stage):
    pairs = []
    for i in range(32):
        y, x, core = i // 8, (i // 2) % 4, i % 2
        if core == stage:
            x = move(x)
        else:
            y = move(y)
        pairs.append((i, (y * 4 + x) * 2 + core))
    return lax.ppermute(value, "cin", pairs)


def after(value, *earlier):
    return lax.optimization_barrier((value, *earlier))[0]


def first_hops(block):
    two = jnp.stack([block, hop(block, lambda at: at ^ 1, 0)])
    return jnp.concatenate([two, hop(two, lambda at: at ^ 3, 0)])


def second_hops(line):
    return [line] + [hop(line, lambda at, shift=shift: (at + shift) % 4, 1) for shift in SHIFTS]


def plane_row(position, second, first, source):
    place = position[1]
    core = place & 1
    along_x, along_y = (place >> 1) & 3, place >> 3
    across = jnp.where(core == 0, along_x ^ PAIRED[first], (along_x + HEARD[second]) & 3)
    down = jnp.where(core == 0, (along_y + HEARD[second]) & 3, along_y ^ PAIRED[first])
    return pl.multiple_of(((down * 4 + across) * 2 + (core ^ source)) * 16, 16)


def tree_row(position, index):
    return pl.multiple_of((position[2] ^ TREE[index]) * 16, 16)


def fetch_plane(position, pieces, source_of, target, sem):
    for second in range(4):
        for first in range(4):
            for source in range(2):
                row = plane_row(position, second, first, source)
                pltpu.make_async_copy(
                    source_of(pieces[second].at[first], source), target(pl.ds(row, 16)), sem
                ).start()


def input_terms(position, w, w_other, *refs):
    pieces, (keep, send, grads, sem) = refs[:4], refs[4:]
    fetch_plane(
        position,
        pieces,
        lambda piece, source: piece.at[source],
        lambda rows: grads.at[:, :, rows, :],
        sem,
    )
    base = (position[1] & 1) * 4
    rows = [pl.ds(tree_row(position, r), 16) for r in range(4)]
    pltpu.make_async_copy(grads, grads, sem).wait()
    for mode in range(4):
        real, imag = (
            jnp.concatenate(
                [block for row in rows for block in (w[base + mode, part, row, :], w_other[mode, part, row, :])],
                axis=0,
            )
            for part in range(2)
        )
        total = jnp.dot(
            jnp.concatenate([real, -imag], axis=0), grads[mode, 0], preferred_element_type=jnp.float32
        ) + jnp.dot(
            jnp.concatenate([imag, real], axis=0), grads[mode, 1], preferred_element_type=jnp.float32
        )
        total = total.reshape(2, 4, 2, 16, 512)
        for part in range(2):
            for r in range(2):
                keep[r, mode, part] = total[part, r]
                send[r, mode, part] = total[part, r + 2]


def weight_terms(position, *refs):
    pieces, late, (x0, x1, x2, here, there, grads, rows, sems) = refs[:4], refs[4:8], refs[8:]
    mode = position[0]
    fetch_plane(
        position,
        pieces,
        lambda piece, source: piece.at[source, mode],
        lambda place: grads.at[0, :, place, :],
        sems.at[0],
    )
    for index, piece in enumerate((x0, x1, x2.at[0], x2.at[1])):
        for source in range(2):
            row = pl.multiple_of(tree_row(position, index) + 64 * source, 16)
            pltpu.make_async_copy(piece.at[source], rows.at[:, :, pl.ds(row, 16), :], sems.at[0]).start()
    fetch_plane(
        position,
        late,
        lambda piece, source: piece.at[:, source],
        lambda place: grads.at[pl.ds(1, 3), :, place, :],
        sems.at[1],
    )
    pltpu.make_async_copy(grads.at[0], grads.at[0], sems.at[0]).wait()
    pltpu.make_async_copy(rows, rows, sems.at[0]).wait()

    total = jnp.zeros((256, 512), jnp.float32)
    contract = (((1,), (1,)), ((), ()))
    for block in range(4):
        if block == 1:
            pltpu.make_async_copy(grads.at[pl.ds(1, 3)], grads.at[pl.ds(1, 3)], sems.at[1]).wait()
        real = rows[block, 0]
        imag = rows[block, 1]
        total += lax.dot_general(
            jnp.concatenate([real, -imag], axis=0), grads[block, 0], contract, preferred_element_type=jnp.float32
        )
        total += lax.dot_general(
            jnp.concatenate([imag, real], axis=0), grads[block, 1], contract, preferred_element_type=jnp.float32
        )
    for part in range(2):
        for source, out in enumerate((here, there)):
            start = part * 128 + source * 64
            out[part] = total[start : start + 64].astype(jnp.bfloat16)


def place_modes(first, position, *refs):
    pieces, (out, staged, read, written) = refs[:-4], refs[-4:]
    reads = [
        pltpu.make_async_copy(piece, staged.at[index], read.at[index]) for index, piece in enumerate(pieces)
    ]
    for copy in reads:
        copy.start()
    for index, copy in enumerate(reads):
        slot, step = (first + index) % 2, (first + index) // 2
        mode = ((position[1] & 1) ^ slot) * 4 + ((position[0] + ARRIVAL[step]) & 3)
        copy.wait()
        pltpu.make_async_copy(staged.at[index], out.at[mode], written).start()
    pltpu.make_async_copy(staged, staged, written).wait()


def place_last(position, piece, placed, out, staged, read, written):
    del placed
    place_modes(7, position, piece, out, staged, read, written)


def place_call(body, name, pieces, position, placed=None):
    held = [] if placed is None else [placed]
    return pl.pallas_call(
        body,
        out_shape=jax.ShapeDtypeStruct((8, 2, 64, 512), jnp.bfloat16),
        in_specs=[SMEM] + [ANY] * (len(pieces) + len(held)),
        out_specs=ANY,
        input_output_aliases={1 + len(pieces): 0} if held else {},
        scratch_shapes=[
            pltpu.VMEM((len(pieces), 2, 64, 512), jnp.bfloat16),
            pltpu.SemaphoreType.DMA((len(pieces),)),
            pltpu.SemaphoreType.DMA,
        ],
        compiler_params=pltpu.CompilerParams(vmem_limit_bytes=8 * MIB),
        cost_estimate=pl.CostEstimate(flops=0, bytes_accessed=2 * MIB, transcendentals=0),
        name=name,
    )(position, *pieces, *held)


def on_device(weight, spectrum, out_grad):
    dp, place, cout = lax.axis_index("dp"), lax.axis_index("cin"), lax.axis_index("cout")
    core = place & 1
    position = jnp.stack([dp, place, cout]).astype(jnp.int32)

    def modes_of(value, start, count):
        return lax.dynamic_slice_in_dim(value, start, count, 0)

    mine, theirs = 4 * core, 4 - 4 * core
    with jax.named_scope("swap_modes"):
        swapped = swap_cores(
            jnp.concatenate([modes_of(v, theirs, 4) for v in (weight, spectrum, out_grad)], axis=2)
        )
        spec = jnp.stack([modes_of(spectrum, mine, 4), swapped[:, :, 64:80]])
        grad = jnp.stack([modes_of(out_grad, mine, 4), swapped[:, :, 80:]])

    with jax.named_scope("gather_grad"):
        line = first_hops(grad)
        held = second_hops(line)

    with jax.named_scope("exchange_modes"):
        exchanged = []
        for shift in SHIFTS:
            at = (dp + shift) & 3
            both = jnp.stack([lax.dynamic_index_in_dim(v, at, 1, False) for v in (spec, grad)])
            exchanged.append(ring(both, "dp", shift))

    with jax.named_scope("gather_rows"):
        xs = jnp.stack(
            [lax.dynamic_index_in_dim(spec, dp, 1, False)] + [block[0] for block in exchanged], axis=1
        )
        xs_across = flip(xs, "cout", 2)
        xs_beside = flip(jnp.stack([xs, xs_across]), "cout", 1)

    with jax.named_scope("gather_late_grad"):
        late = jnp.stack([block[1] for block in exchanged])
        late_line = first_hops(late)

    tree = jax.ShapeDtypeStruct((2, 4, 2, 2, 16, 512), jnp.float32)
    keep, send = pl.pallas_call(
        input_terms,
        out_shape=(tree, tree),
        in_specs=[SMEM, VMEM, VMEM] + [ANY] * 4,
        out_specs=(VMEM, VMEM),
        scratch_shapes=[pltpu.VMEM((4, 2, 512, 512), jnp.bfloat16), pltpu.SemaphoreType.DMA],
        compiler_params=pltpu.CompilerParams(vmem_limit_bytes=24 * MIB),
        cost_estimate=pl.CostEstimate(flops=1 << 30, bytes_accessed=8 * MIB, transcendentals=0),
        name="input_terms",
    )(position, weight, swapped, *held)
    with jax.named_scope("sum_input"):
        beside = flip(after(send, xs_across), "cout", 1)
        across = flip(keep[1] + beside[1], "cout", 2)
        summed = ((keep[0] + beside[0]) + across).astype(jnp.bfloat16)
        own, other = summed[:, :, 0], swap_cores(summed[:, :, 1])
        spectrum_grad = jnp.where(
            core == 0, jnp.concatenate([own, other], axis=0), jnp.concatenate([other, own], axis=0)
        )

    with jax.named_scope("gather_late_grad"):
        late_held = second_hops(late_line)
    here, there = pl.pallas_call(
        weight_terms,
        out_shape=[jax.ShapeDtypeStruct((2, 64, 512), jnp.bfloat16)] * 2,
        in_specs=[SMEM] + [ANY] * 11,
        out_specs=[VMEM] * 2,
        scratch_shapes=[
            pltpu.VMEM((4, 2, 512, 512), jnp.bfloat16),
            pltpu.VMEM((4, 2, 128, 512), jnp.bfloat16),
            pltpu.SemaphoreType.DMA((2,)),
        ],
        compiler_params=pltpu.CompilerParams(vmem_limit_bytes=24 * MIB),
        cost_estimate=pl.CostEstimate(flops=1 << 30, bytes_accessed=5 * MIB, transcendentals=0),
        name="weight_terms",
    )(position, *held, *late_held, xs, xs_across, xs_beside)

    with jax.named_scope("spread_weight"):
        back_0, ahead_0 = ring(here, "dp", 1), ring(here, "dp", 3)
        other = swap_cores(there)
        back_1, ahead_1 = ring(other, "dp", 1), ring(other, "dp", 3)
        far_0, far_1 = ring(back_0, "dp", 1), ring(ahead_1, "dp", 3)
    placed = place_call(
        functools.partial(place_modes, 0),
        "place_modes",
        [here, other, back_0, back_1, ahead_0, ahead_1, far_0],
        position,
    )
    weight_grad = place_call(place_last, "place_last", [far_1], after(position, spectrum_grad), placed)
    return (spectrum_grad, weight_grad)


def solution(mesh):
    placed = (
        P(None, None, "cin", "cout"),
        P(None, None, ("cin", "cout"), "dp"),
        P(None, None, ("cout", "cin"), "dp"),
    )
    return jax.shard_map(
        on_device,
        mesh=mesh,
        in_specs=placed,
        out_specs=(P(None, None, ("cin", "cout"), "dp"), P(None, None, "cin", "cout")),
        check_vma=False,
    )
```
